32 devices in a mesh: gz: 16 (over z, y, core), ta: 2 (over x).
Axes of the slice: x: 2, y: 2, z: 4, core: 2. Of those that a mesh axis runs over, the one named last changes fastest.
Arguments:
- e_field: float32 [3, 32, 1024, 128], P(None, 'ta', 'gz'), may hold values from -6 to 6
- h_field: float32 [3, 32, 1024, 128], P(None, 'ta', 'gz'), may hold values from -6 to 6
- polar: float32 [3, 32, 1024, 128], P(None, 'ta', 'gz'), may hold values from -6 to 6
- polar_rate: float32 [3, 32, 1024, 128], P(None, 'ta', 'gz'), may hold values from -6 to 6
- material: int32 [32, 1024, 128], P('ta', 'gz'), may hold values 0 or 1
- shift_counts: int32 [2], replicated, may hold values from 1 to 32, as said below
Outputs:
- e_final: float32 [3, 32, 1024, 128], P(None, 'ta', 'gz')
- h_final: float32 [3, 32, 1024, 128], P(None, 'ta', 'gz')
- polar_final: float32 [3, 32, 1024, 128], P(None, 'ta', 'gz')
The draws below stay inside these ranges and needn't reach their ends.
Inputs may be any that keep to these rules, and one draw needn't show every extreme that they name: `shift_counts`: every entry is at least 1 and at most 32, and at least one entry equals 32.
All inputs are finite; a program needn't handle non-finite values. No bound on the sum of `material` on one device may be relied on, other than what follows from the above.
Results may differ from the reference program's by a relative error of at most 0.0001.
Values sent between devices are 32-bit elements; how exact they have to be, the bound alone decides.
A program may use at most 64 MiB of HBM per device.

```python
import jax
import jax.numpy as jnp
from jax import lax

NY = 128
SMAX = 32
STEPS = 4
CYCLES = 2
NX = 32
NZ = 1024


def draw_shift_counts(key, part):
    key = jax.random.fold_in(key, 7)
    others = jax.random.randint(key, (CYCLES,), 1, SMAX)
    chosen = jax.random.randint(jax.random.fold_in(key, 1), (), 0, CYCLES)
    return jnp.where(jnp.arange(CYCLES) == chosen, SMAX, others).astype(jnp.int32)


def touch_ends(entries, own_key, low, largest):
    spot = [jax.random.randint(jax.random.fold_in(own_key, axis), (), 0, length) for axis, length in enumerate(entries.shape)]
    widest = entries.shape.index(max(entries.shape))
    neighbour = spot[:widest] + [(spot[widest] + 1) % entries.shape[widest]] + spot[widest + 1:]
    return entries.at[tuple(spot)].set(low).at[tuple(neighbour)].set(largest)


def block_levels(own_key, dims, shards, smallest, largest):
    factor_of, own = 1.0, jax.random.fold_in(own_key, 6)
    for position, blocks in shards:
        draws = jnp.exp(jax.random.uniform(jax.random.fold_in(own, position), (blocks,), jnp.float32, smallest / len(shards), largest / len(shards)))
        factor_of = factor_of * jnp.repeat(draws, dims[position] // blocks).reshape([-1 if axis == position else 1 for axis in range(len(dims))])
    return factor_of


def centred(own_key, extent, deviation, bound, shards=(), dtype=jnp.bfloat16):
    array = deviation * jax.random.normal(own_key, extent, jnp.float32)
    if shards:
        array = array * block_levels(own_key, extent, shards, -0.22, 0.18)
    return jnp.clip(array, -bound, bound).astype(dtype)


def setup_inputs(seed: int = 0) -> dict:
    key_of = jax.random.split(jax.random.key(seed), 7)
    return {
        "e_field": centred(key_of[0], (3, NX, NZ, NY), 1.0, 6.0, ((1, 2), (2, 16)), jnp.float32),
        "h_field": centred(key_of[1], (3, NX, NZ, NY), 1.0, 6.0, ((1, 2), (2, 16)), jnp.float32),
        "polar": centred(key_of[2], (3, NX, NZ, NY), 1.0, 6.0, ((1, 2), (2, 16)), jnp.float32),
        "polar_rate": centred(key_of[3], (3, NX, NZ, NY), 1.0, 6.0, ((1, 2), (2, 16)), jnp.float32),
        "material": touch_ends((jax.random.randint(key_of[4], (NX, NZ, NY), 0, 3) < 1).astype(jnp.int32), jax.random.fold_in(key_of[4], 1), 0, 1),
        "shift_counts": draw_shift_counts(jax.random.fold_in(key_of[6], 71), 0),
    }


time_step = 0.5


def material_terms(material):
    core = material == 1
    eps_inf = jnp.where(core, 11.7, 2.1).astype(jnp.float32)
    delta = jnp.where(core, 0.5, 0.2).astype(jnp.float32)
    omega_sq = jnp.where(core, 1.44, 4.0).astype(jnp.float32)
    damping = jnp.where(core, 0.05, 0.2).astype(jnp.float32)
    kerr = jnp.where(core, 0.05, 0.01).astype(jnp.float32)
    return eps_inf, delta, omega_sq, damping, kerr


def forward_diff(field, axis):
    width = field.shape[axis]
    upper = jnp.concatenate([lax.slice_in_dim(field, 1, width, axis=axis), jnp.zeros_like(lax.slice_in_dim(field, 0, 1, axis=axis))], axis)
    return upper - field


def backward_diff(field, axis):
    width = field.shape[axis]
    lower = jnp.concatenate([jnp.zeros_like(lax.slice_in_dim(field, 0, 1, axis=axis)), lax.slice_in_dim(field, 0, width - 1, axis=axis)], axis)
    return field - lower


def curl_forward(field):
    curl_x = forward_diff(field[2], 2) - forward_diff(field[1], 1)
    curl_y = forward_diff(field[0], 1) - forward_diff(field[2], 0)
    curl_z = forward_diff(field[1], 0) - forward_diff(field[0], 2)
    return jnp.stack([curl_x, curl_y, curl_z])


def curl_backward(field):
    curl_x = backward_diff(field[2], 2) - backward_diff(field[1], 1)
    curl_y = backward_diff(field[0], 1) - backward_diff(field[2], 0)
    curl_z = backward_diff(field[1], 0) - backward_diff(field[0], 2)
    return jnp.stack([curl_x, curl_y, curl_z])


def advance(field, count):
    padded = jnp.pad(field, ((0, 0), (0, 0), (0, SMAX), (0, 0)))
    return lax.dynamic_slice_in_dim(padded, count.astype(jnp.int32), NZ, 2)


def reference(e_field, h_field, polar, polar_rate, material, shift_counts):
    eps_inf, delta, omega_sq, damping, kerr = material_terms(material)
    for cycle in range(CYCLES):
        for step in range(STEPS):
            h_field = h_field - time_step * curl_forward(e_field)
            polar_rate = polar_rate + time_step * (omega_sq * (delta * e_field - polar) - damping * polar_rate)
            polar = polar + time_step * polar_rate
            intensity = jnp.sum(e_field * e_field, axis=0)
            e_field = e_field + time_step * (curl_backward(h_field) - polar_rate) / (eps_inf * (1.0 + kerr * intensity))
        count = shift_counts[cycle]
        e_field = advance(e_field, count)
        h_field = advance(h_field, count)
        polar = advance(polar, count)
        polar_rate = advance(polar_rate, count)
    return e_field, h_field, polar
```

```python
import functools

import jax
import jax.numpy as jnp
from jax import lax
from jax.experimental import pallas as pl
from jax.experimental.pallas import tpu as pltpu
from jax.sharding import PartitionSpec as P

SMAX = 32
STEPS = 4
CYCLES = 2
TOTAL = STEPS * CYCLES
HALO = 8
PAD = 8
BELOW = SMAX + HALO
OWN = PAD + HALO
DT = 0.5
MESH = pl.DeviceIdType.MESH


def kernel(rows_sent, e_in, h_in, p_in, q_in, m_in, counts, e_out, h_out, p_out,
           f, q, got, joined, made, mat, own_mat, left_e, right_e, left_h, masks,
           load_sem, zs_sem, zr_sem, xls, xlr, xrs, xrr, hs, hr, fs, fr, out_sem):
    nx, nz, ny = m_in.shape
    end = OWN + nz
    lo, hi = PAD, end + HALO
    span = hi - lo
    gz, ta = lax.axis_index("gz"), lax.axis_index("ta")
    ngz, nta = lax.axis_size("gz"), lax.axis_size("ta")
    has_dn, has_up = gz > 0, gz < ngz - 1
    has_l, has_r = ta > 0, ta < nta - 1
    dn, up = {"gz": gz - 1}, {"gz": gz + 1}
    lt, rt = {"ta": ta - 1}, {"ta": ta + 1}
    s0, s1 = jnp.clip(counts[0], 1, SMAX), jnp.clip(counts[1], 1, SMAX)
    total = jnp.clip(s0 + s1, SMAX, CYCLES * SMAX)

    loads = [
        pltpu.make_async_copy(e_in, f.at[0:3, :, OWN:end, :], load_sem.at[0]),
        pltpu.make_async_copy(h_in, f.at[3:6, :, OWN:end, :], load_sem.at[1]),
        pltpu.make_async_copy(p_in, f.at[6:9, :, OWN:end, :], load_sem.at[2]),
        pltpu.make_async_copy(q_in, q.at[:, :, OWN:end, :], load_sem.at[3]),
        pltpu.make_async_copy(m_in, own_mat.at[:, BELOW:BELOW + nz, :], load_sem.at[4]),
    ]
    for copy in loads:
        copy.start()

    barrier = pltpu.get_barrier_semaphore()
    around = ((has_dn, dn), (has_up, up), (has_l, lt), (has_r, rt))
    for there, device in around:
        @pl.when(there)
        def _():
            pl.semaphore_signal(barrier, inc=1, device_id=device, device_id_type=MESH)
    pl.semaphore_wait(barrier, sum(there.astype(jnp.int32) for there, _ in around))

    def remote(src, dst, send, recv, device):
        return pltpu.make_async_remote_copy(src_ref=src, dst_ref=dst, send_sem=send, recv_sem=recv,
                                            device_id=device, device_id_type=MESH)

    down, upward = [], []
    for k, (src, dst) in enumerate(((e_in, f.at[0:3]), (h_in, f.at[3:6]), (p_in, f.at[6:9]), (q_in, q))):
        down.append(remote(src.at[:, :, 0:HALO, :], dst.at[:, :, end:hi, :], zs_sem.at[0, k], zr_sem.at[0, k], dn))
        upward.append(remote(src.at[:, :, nz - HALO:nz, :], dst.at[:, :, lo:OWN, :], zs_sem.at[1, k], zr_sem.at[1, k], up))
    down.append(remote(m_in.at[:, 0:HALO, :], own_mat.at[:, BELOW + nz:BELOW + nz + HALO, :], zs_sem.at[0, 4], zr_sem.at[0, 4], dn))
    upward.append(remote(m_in.at[:, nz - BELOW:nz, :], own_mat.at[:, 0:BELOW, :], zs_sem.at[1, 4], zr_sem.at[1, 4], up))

    @pl.when(has_dn)
    def _():
        for copy in down:
            copy.start()

    @pl.when(has_up)
    def _():
        for copy in upward:
            copy.start()

    def clear(ref, *index):
        shape = ref.at[index].shape
        ref[index] = jnp.zeros(shape, ref.dtype)

    every = slice(None)

    def edge_rows(first, last):
        def body(x, carry):
            f[:, x, first:last, :] = jnp.zeros((9, last - first, ny), jnp.float32)
            q[:, x, first:last, :] = jnp.zeros((3, last - first, ny), jnp.float32)
            return carry
        lax.fori_loop(0, nx, body, 0)

    edge_rows(0, lo)
    edge_rows(hi, hi + PAD)

    @pl.when(jnp.logical_not(has_dn))
    def _():
        edge_rows(lo, OWN)
        def body(x, carry):
            own_mat[x, 0:BELOW, :] = jnp.zeros((BELOW, ny), jnp.int32)
            return carry
        lax.fori_loop(0, nx, body, 0)

    @pl.when(jnp.logical_not(has_up))
    def _():
        edge_rows(end, hi)
        def body(x, carry):
            own_mat[x, BELOW + nz:BELOW + nz + HALO, :] = jnp.zeros((HALO, ny), jnp.int32)
            got[:, x] = jnp.zeros(got.at[:, x].shape, jnp.float32)
            return carry
        lax.fori_loop(0, nx, body, 0)

    def clear_slot(t, carry):
        left_e[t, :, span:span + PAD, :] = jnp.zeros((3, PAD, ny), jnp.float32)

        @pl.when(jnp.logical_not(has_l))
        def _():
            left_e[t, :, 0:span, :] = jnp.zeros((3, span, ny), jnp.float32)

        @pl.when(jnp.logical_not(has_r))
        def _():
            right_e[t] = jnp.zeros((2, span, ny), jnp.float32)
        return carry
    lax.fori_loop(0, TOTAL, clear_slot, 0)

    @pl.when(jnp.logical_not(has_l))
    def _():
        left_h[...] = jnp.zeros(left_h.shape, jnp.float32)

    for copy in loads:
        copy.wait()

    @pl.when(has_dn)
    def _():
        for copy in down:
            copy.wait_send()
        for copy in upward:
            copy.wait_recv()

    @pl.when(has_up)
    def _():
        for copy in upward:
            copy.wait_send()
        for copy in down:
            copy.wait_recv()

    def to_left(t):
        return remote(f.at[1:3, 0, lo:hi, :], right_e.at[t], xls.at[t], xlr.at[t], lt)

    def to_right(t):
        return remote(f.at[0:3, nx - 1, lo:hi, :], left_e.at[t, :, 0:span, :], xrs.at[t], xrr.at[t], rt)

    first_h = remote(f.at[4:6, nx - 1, lo:hi, :], left_h, hs, hr, rt)

    def start_left(t):
        @pl.when(has_l)
        def _():
            to_left(t).start()

    def start_right(t):
        @pl.when(has_r)
        def _():
            to_right(t).start()

    def wait_x(t):
        @pl.when(has_l)
        def _():
            to_left(t).wait_send()
            to_right(t).wait_recv()

        @pl.when(has_r)
        def _():
            to_right(t).wait_send()
            to_left(t).wait_recv()

    start_left(0)
    start_right(0)

    @pl.when(has_r)
    def _():
        first_h.start()
        first_h.wait_send()

    @pl.when(has_l)
    def _():
        first_h.wait_recv()

    lane = lax.broadcasted_iota(jnp.int32, (8, ny), 1)
    row = lax.broadcasted_iota(jnp.int32, (8, ny), 0)
    starts = list(range(lo, hi, 8))

    def y_up(v):
        return jnp.where(lane < ny - 1, pltpu.roll(v, ny - 1, 1), 0.0)

    def y_down(v):
        return jnp.where(lane > 0, pltpu.roll(v, 1, 1), 0.0)

    def new_cycle(shift):
        low = shift
        high = ngz * nz + shift
        for r in starts:
            place = gz * nz + (r - OWN) + row
            masks[0, r:r + 8, :] = jnp.where(place - 1 >= low, 1.0, 0.0)
            masks[1, r:r + 8, :] = jnp.where(place < high, DT, 0.0)

        def body(x, carry):
            for r in starts:
                mat[x, r:r + 8, :] = own_mat[x, pl.ds(SMAX - shift + (r - lo), 8), :]
            return carry
        lax.fori_loop(0, nx, body, 0)

    def h_plane(x, after):
        for r in starts:
            ex, ey, ez = (f[c, x, r:r + 8, :] for c in range(3))
            ex_z, ey_z = (f[c, x, r + 1:r + 9, :] for c in range(2))
            ey_x, ez_x = after(0, r), after(1, r)
            f[3, x, r:r + 8, :] -= DT * ((y_up(ez) - ez) - (ey_z - ey))
            f[4, x, r:r + 8, :] -= DT * ((ex_z - ex) - (ez_x - ez))
            f[5, x, r:r + 8, :] -= DT * ((ey_x - ey) - (y_up(ex) - ex))

    def next_plane(x):
        return lambda c, r: f[1 + c, x + 1, r:r + 8, :]

    def e_plane(x, before):
        for r in starts:
            hx, hy, hz = (f[3 + c, x, r:r + 8, :] for c in range(3))
            keep = masks[0, r:r + 8, :]
            hx_z = f[3, x, r - 1:r + 7, :] * keep
            hy_z = f[4, x, r - 1:r + 7, :] * keep
            hy_x, hz_x = before(0, r), before(1, r)
            curl = (
                (hz - y_down(hz)) - (hy - hy_z),
                (hx - hx_z) - (hz - hz_x),
                (hy - hy_x) - (hx - y_down(hx)),
            )
            core = mat[x, r:r + 8, :] == 1
            keep_rate = jnp.where(core, 1.0 - DT * 0.05, 1.0 - DT * 0.2)
            drive = jnp.where(core, DT * 1.44 * 0.5, DT * 4.0 * 0.2)
            spring = jnp.where(core, DT * 1.44, DT * 4.0)
            eps = jnp.where(core, 11.7, 2.1)
            bend = jnp.where(core, 11.7 * 0.05, 2.1 * 0.01)
            e = [f[c, x, r:r + 8, :] for c in range(3)]
            intensity = e[0] * e[0] + e[1] * e[1] + e[2] * e[2]
            gain = masks[1, r:r + 8, :] / (eps + bend * intensity)
            for c in range(3):
                p = f[6 + c, x, r:r + 8, :]
                rate = keep_rate * q[c, x, r:r + 8, :] + (drive * e[c] - spring * p)
                q[c, x, r:r + 8, :] = rate
                f[6 + c, x, r:r + 8, :] = p + DT * rate
                f[c, x, r:r + 8, :] = e[c] + gain * (curl[c] - rate)

    def previous_plane(x):
        return lambda c, r: f[4 + c, x - 1, r:r + 8, :]

    def final(x):
        return remote(f.at[:, x, OWN:OWN + rows_sent, :], got.at[:, x, 0:rows_sent, :], fs.at[x], fr.at[x], dn)

    def done(t, x):
        @pl.when(jnp.logical_and(t == TOTAL - 1, has_dn))
        def _():
            final(x).start()

    last = nx - 1

    def step(t, carry):
        @pl.when(t == 0)
        def _():
            new_cycle(jnp.int32(0))

        @pl.when(t == STEPS)
        def _():
            new_cycle(s0)

        wait_x(t)

        @pl.when(has_l)
        def _():
            for r in starts:
                k = r - lo
                ex, ey, ez = (left_e[t, c, k:k + 8, :] for c in range(3))
                ex_z = left_e[t, 0, k + 1:k + 9, :]
                ey_x, ez_x = (f[c, 0, r:r + 8, :] for c in (1, 2))
                left_h[0, k:k + 8, :] -= DT * ((ex_z - ex) - (ez_x - ez))
                left_h[1, k:k + 8, :] -= DT * ((ey_x - ey) - (y_up(ex) - ex))

        h_plane(last - 1, next_plane(last - 1))
        h_plane(last, lambda c, r: right_e[t, c, r - lo:r - lo + 8, :])
        e_plane(last, previous_plane(last))

        @pl.when(t < TOTAL - 1)
        def _():
            start_right(t + 1)
        done(t, last)

        h_plane(0, next_plane(0))
        e_plane(0, lambda c, r: left_h[c, r - lo:r - lo + 8, :])

        @pl.when(t < TOTAL - 1)
        def _():
            start_left(t + 1)
        done(t, 0)

        def inner(x, c):
            h_plane(x, next_plane(x))
            e_plane(x, previous_plane(x))
            done(t, x)
            return c
        lax.fori_loop(1, last - 1, inner, 0)
        e_plane(last - 1, previous_plane(last - 1))
        done(t, last - 1)
        return carry

    lax.fori_loop(0, TOTAL, step, 0)

    @pl.when(jnp.logical_not(has_up))
    def _():
        def body(x, carry):
            got[:, x, 0:HALO, :] = f[:, x, end:hi, :]
            return carry
        lax.fori_loop(0, nx, body, 0)

    outs = (e_out, h_out, p_out)

    def leave(x):
        return [pltpu.make_async_copy(made.at[3 * k:3 * k + 3, x], outs[k].at[:, x], out_sem.at[k, x]) for k in range(3)]

    def assemble(n, carry):
        x = jnp.where(n == 0, last, n - 1)

        @pl.when(has_up)
        def _():
            final(x).wait_recv()
        for c in range(9):
            joined[c, 0:SMAX, :] = f[c, x, end - SMAX:end, :]
            joined[c, SMAX:SMAX + rows_sent, :] = got[c, x, 0:rows_sent, :]
        for c in range(9):
            for k in range(0, nz, 8):
                made[c, x, k:k + 8, :] = joined[c, pl.ds(total + (SMAX - nz) + k, 8), :]
        for copy in leave(x):
            copy.start()
        return carry

    lax.fori_loop(0, nx, assemble, 0)

    def finish(x, carry):
        for copy in leave(x):
            copy.wait()

        @pl.when(has_dn)
        def _():
            final(x).wait_send()
        return carry
    lax.fori_loop(0, nx, finish, 0)


def run(rows_sent, collective, e_field, h_field, polar, polar_rate, material, shift_counts):
    nx, nz, ny = material.shape
    span = nz + 2 * HALO
    tall = span + 2 * PAD
    f32 = jnp.float32
    dma = pltpu.SemaphoreType.DMA
    anywhere = pl.BlockSpec(memory_space=pl.ANY)
    return pl.pallas_call(
        functools.partial(kernel, rows_sent),
        out_shape=[jax.ShapeDtypeStruct(e_field.shape, f32)] * 3,
        in_specs=[anywhere] * 5 + [pl.BlockSpec(memory_space=pltpu.SMEM)],
        out_specs=[anywhere] * 3,
        scratch_shapes=[
            pltpu.VMEM((9, nx, tall, ny), f32),
            pltpu.VMEM((3, nx, tall, ny), f32),
            pltpu.VMEM((9, nx, nz, ny), f32),
            pltpu.VMEM((9, SMAX + nz, ny), f32),
            pltpu.VMEM((9, nx, nz, ny), f32),
            pltpu.VMEM((nx, tall, ny), jnp.int32),
            pltpu.VMEM((nx, BELOW + nz + HALO, ny), jnp.int32),
            pltpu.VMEM((TOTAL, 3, span + PAD, ny), f32),
            pltpu.VMEM((TOTAL, 2, span, ny), f32),
            pltpu.VMEM((2, span, ny), f32),
            pltpu.VMEM((2, tall, ny), f32),
            dma((5,)), dma((2, 5)), dma((2, 5)),
            dma((TOTAL,)), dma((TOTAL,)), dma((TOTAL,)), dma((TOTAL,)),
            dma, dma,
            dma((nx,)), dma((nx,)), dma((3, nx)),
        ],
        compiler_params=pltpu.CompilerParams(
            collective_id=collective, has_side_effects=True, vmem_limit_bytes=52 * 1024 * 1024),
    )(e_field, h_field, polar, polar_rate, material, shift_counts)


def local(e_field, h_field, polar, polar_rate, material, shift_counts):
    nz = material.shape[1]
    return tuple(run(nz, 0, e_field, h_field, polar, polar_rate, material, shift_counts))


def solution(mesh):
    placed = (
        P(None, "ta", "gz", None),
        P(None, "ta", "gz", None),
        P(None, "ta", "gz", None),
        P(None, "ta", "gz", None),
        P("ta", "gz", None),
        P(),
    )
    return jax.shard_map(
        local,
        mesh=mesh,
        in_specs=placed,
        out_specs=(P(None, "ta", "gz", None), P(None, "ta", "gz", None), P(None, "ta", "gz", None)),
        check_vma=False,
    )
```

```python
import functools

import jax
import jax.numpy as jnp
from jax import lax
from jax.experimental import pallas as pl
from jax.experimental.pallas import tpu as pltpu
from jax.sharding import PartitionSpec as P

SMAX = 32
STEPS = 4
CYCLES = 2
TOTAL = STEPS * CYCLES
HALO = 8
PAD = 8
BELOW = SMAX + HALO
OWN = PAD + HALO
DT = 0.5
MESH = pl.DeviceIdType.MESH


def kernel(rows_sent, e_in, h_in, p_in, q_in, m_in, counts, e_out, h_out, p_out,
           f, q, got, joined, made, mat, own_mat, late_mat, left_e, right_e, left_h, masks,
           load_sem, zs_sem, zr_sem, xls, xlr, xrs, xrr, hs, hr, ms, mr, fs, fr, out_sem):
    nx, nz, ny = m_in.shape
    end = OWN + nz
    lo, hi = PAD, end + HALO
    span = hi - lo
    gz, ta = lax.axis_index("gz"), lax.axis_index("ta")
    ngz, nta = lax.axis_size("gz"), lax.axis_size("ta")
    has_dn, has_up = gz > 0, gz < ngz - 1
    has_l, has_r = ta > 0, ta < nta - 1
    dn, up = {"gz": gz - 1}, {"gz": gz + 1}
    lt, rt = {"ta": ta - 1}, {"ta": ta + 1}
    s0, s1 = jnp.clip(counts[0], 1, SMAX), jnp.clip(counts[1], 1, SMAX)
    total = jnp.clip(s0 + s1, SMAX, CYCLES * SMAX)

    loads = [
        pltpu.make_async_copy(e_in, f.at[0:3, :, OWN:end, :], load_sem.at[0]),
        pltpu.make_async_copy(h_in, f.at[3:6, :, OWN:end, :], load_sem.at[1]),
        pltpu.make_async_copy(p_in, f.at[6:9, :, OWN:end, :], load_sem.at[2]),
        pltpu.make_async_copy(q_in, q.at[:, :, OWN:end, :], load_sem.at[3]),
        pltpu.make_async_copy(m_in, own_mat.at[:, BELOW:BELOW + nz, :], load_sem.at[4]),
    ]
    for copy in loads:
        copy.start()

    barrier = pltpu.get_barrier_semaphore()
    around = ((has_dn, dn), (has_up, up), (has_l, lt), (has_r, rt))
    for there, device in around:
        @pl.when(there)
        def _():
            pl.semaphore_signal(barrier, inc=1, device_id=device, device_id_type=MESH)
    pl.semaphore_wait(barrier, sum(there.astype(jnp.int32) for there, _ in around))

    def remote(src, dst, send, recv, device):
        return pltpu.make_async_remote_copy(src_ref=src, dst_ref=dst, send_sem=send, recv_sem=recv,
                                            device_id=device, device_id_type=MESH)

    down, upward = [], []
    for k, (src, dst) in enumerate(((e_in, f.at[0:3]), (h_in, f.at[3:6]), (p_in, f.at[6:9]), (q_in, q))):
        down.append(remote(src.at[:, :, 0:HALO, :], dst.at[:, :, end:hi, :], zs_sem.at[0, k], zr_sem.at[0, k], dn))
        upward.append(remote(src.at[:, :, nz - HALO:nz, :], dst.at[:, :, lo:OWN, :], zs_sem.at[1, k], zr_sem.at[1, k], up))
    down.append(remote(m_in.at[:, 0:HALO, :], own_mat.at[:, BELOW + nz:BELOW + nz + HALO, :], zs_sem.at[0, 4], zr_sem.at[0, 4], dn))
    upward.append(remote(m_in.at[:, nz - HALO:nz, :], own_mat.at[:, SMAX:BELOW, :], zs_sem.at[1, 4], zr_sem.at[1, 4], up))
    later = remote(m_in.at[:, nz - BELOW:nz - HALO, :], late_mat, ms, mr, up)

    @pl.when(has_dn)
    def _():
        for copy in down:
            copy.start()

    @pl.when(has_up)
    def _():
        for copy in upward:
            copy.start()
        later.start()

    def edge_rows(first, last):
        def body(x, carry):
            f[:, x, first:last, :] = jnp.zeros((9, last - first, ny), jnp.float32)
            q[:, x, first:last, :] = jnp.zeros((3, last - first, ny), jnp.float32)
            return carry
        lax.fori_loop(0, nx, body, 0)

    edge_rows(0, lo)
    edge_rows(hi, hi + PAD)

    @pl.when(jnp.logical_not(has_dn))
    def _():
        edge_rows(lo, OWN)
        def body(x, carry):
            own_mat[x, 0:BELOW, :] = jnp.zeros((BELOW, ny), jnp.int32)
            late_mat[x] = jnp.zeros((SMAX, ny), jnp.int32)
            return carry
        lax.fori_loop(0, nx, body, 0)

    @pl.when(jnp.logical_not(has_up))
    def _():
        edge_rows(end, hi)
        def body(x, carry):
            own_mat[x, BELOW + nz:BELOW + nz + HALO, :] = jnp.zeros((HALO, ny), jnp.int32)
            got[:, x] = jnp.zeros(got.at[:, x].shape, jnp.float32)
            return carry
        lax.fori_loop(0, nx, body, 0)

    def clear_slot(t, carry):
        left_e[t, :, span:span + PAD, :] = jnp.zeros((3, PAD, ny), jnp.float32)

        @pl.when(jnp.logical_not(has_l))
        def _():
            left_e[t, :, 0:span, :] = jnp.zeros((3, span, ny), jnp.float32)

        @pl.when(jnp.logical_not(has_r))
        def _():
            right_e[t] = jnp.zeros((2, span, ny), jnp.float32)
        return carry
    lax.fori_loop(0, TOTAL, clear_slot, 0)

    @pl.when(jnp.logical_not(has_l))
    def _():
        left_h[...] = jnp.zeros(left_h.shape, jnp.float32)

    for copy in loads:
        copy.wait()

    @pl.when(has_dn)
    def _():
        for copy in down:
            copy.wait_send()
        for copy in upward:
            copy.wait_recv()

    @pl.when(has_up)
    def _():
        for copy in upward:
            copy.wait_send()
        for copy in down:
            copy.wait_recv()

    def to_left(t):
        return remote(f.at[1:3, 0, lo:hi, :], right_e.at[t], xls.at[t], xlr.at[t], lt)

    def to_right(t):
        return remote(f.at[0:3, nx - 1, lo:hi, :], left_e.at[t, :, 0:span, :], xrs.at[t], xrr.at[t], rt)

    first_h = remote(f.at[4:6, nx - 1, lo:hi, :], left_h, hs, hr, rt)

    def start_left(t):
        @pl.when(has_l)
        def _():
            to_left(t).start()

    def start_right(t):
        @pl.when(has_r)
        def _():
            to_right(t).start()

    def wait_x(t):
        @pl.when(has_l)
        def _():
            to_left(t).wait_send()
            to_right(t).wait_recv()

        @pl.when(has_r)
        def _():
            to_right(t).wait_send()
            to_left(t).wait_recv()

    start_left(0)
    start_right(0)

    @pl.when(has_r)
    def _():
        first_h.start()
        first_h.wait_send()

    @pl.when(has_l)
    def _():
        first_h.wait_recv()

    lane = lax.broadcasted_iota(jnp.int32, (8, ny), 1)
    row = lax.broadcasted_iota(jnp.int32, (8, ny), 0)
    starts = list(range(lo, hi, 8))

    def y_up(v):
        return jnp.where(lane < ny - 1, pltpu.roll(v, ny - 1, 1), 0.0)

    def y_down(v):
        return jnp.where(lane > 0, pltpu.roll(v, 1, 1), 0.0)

    def new_cycle(shift):
        low = shift
        high = ngz * nz + shift
        for r in starts:
            place = gz * nz + (r - OWN) + row
            masks[0, r:r + 8, :] = jnp.where(place - 1 >= low, 1.0, 0.0)
            masks[1, r:r + 8, :] = jnp.where(place < high, DT, 0.0)

        def body(x, carry):
            for r in starts:
                mat[x, r:r + 8, :] = own_mat[x, pl.ds(SMAX - shift + (r - lo), 8), :]
            return carry
        lax.fori_loop(0, nx, body, 0)

    def h_plane(x, after):
        for r in starts:
            ex, ey, ez = (f[c, x, r:r + 8, :] for c in range(3))
            ex_z, ey_z = (f[c, x, r + 1:r + 9, :] for c in range(2))
            ey_x, ez_x = after(0, r), after(1, r)
            f[3, x, r:r + 8, :] -= DT * ((y_up(ez) - ez) - (ey_z - ey))
            f[4, x, r:r + 8, :] -= DT * ((ex_z - ex) - (ez_x - ez))
            f[5, x, r:r + 8, :] -= DT * ((ey_x - ey) - (y_up(ex) - ex))

    def next_plane(x):
        return lambda c, r: f[1 + c, x + 1, r:r + 8, :]

    def e_plane(x, before):
        for r in starts:
            hx, hy, hz = (f[3 + c, x, r:r + 8, :] for c in range(3))
            keep = masks[0, r:r + 8, :]
            hx_z = f[3, x, r - 1:r + 7, :] * keep
            hy_z = f[4, x, r - 1:r + 7, :] * keep
            hy_x, hz_x = before(0, r), before(1, r)
            curl = (
                (hz - y_down(hz)) - (hy - hy_z),
                (hx - hx_z) - (hz - hz_x),
                (hy - hy_x) - (hx - y_down(hx)),
            )
            core = mat[x, r:r + 8, :] == 1
            keep_rate = jnp.where(core, 1.0 - DT * 0.05, 1.0 - DT * 0.2)
            drive = jnp.where(core, DT * 1.44 * 0.5, DT * 4.0 * 0.2)
            spring = jnp.where(core, DT * 1.44, DT * 4.0)
            eps = jnp.where(core, 11.7, 2.1)
            bend = jnp.where(core, 11.7 * 0.05, 2.1 * 0.01)
            e = [f[c, x, r:r + 8, :] for c in range(3)]
            intensity = e[0] * e[0] + e[1] * e[1] + e[2] * e[2]
            gain = masks[1, r:r + 8, :] / (eps + bend * intensity)
            for c in range(3):
                p = f[6 + c, x, r:r + 8, :]
                rate = keep_rate * q[c, x, r:r + 8, :] + (drive * e[c] - spring * p)
                q[c, x, r:r + 8, :] = rate
                f[6 + c, x, r:r + 8, :] = p + DT * rate
                f[c, x, r:r + 8, :] = e[c] + gain * (curl[c] - rate)

    def previous_plane(x):
        return lambda c, r: f[4 + c, x - 1, r:r + 8, :]

    def final(x):
        return remote(f.at[:, x, OWN:OWN + rows_sent, :], got.at[:, x, 0:rows_sent, :], fs.at[x], fr.at[x], dn)

    def done(t, x):
        @pl.when(jnp.logical_and(t == TOTAL - 1, has_dn))
        def _():
            final(x).start()

    last = nx - 1

    def step(t, carry):
        @pl.when(t == 0)
        def _():
            new_cycle(jnp.int32(0))

        @pl.when(t == STEPS)
        def _():
            @pl.when(has_up)
            def _():
                later.wait_send()

            @pl.when(has_dn)
            def _():
                later.wait_recv()

            def body(x, c):
                own_mat[x, 0:SMAX, :] = late_mat[x]
                return c
            lax.fori_loop(0, nx, body, 0)
            new_cycle(s0)

        wait_x(t)

        @pl.when(has_l)
        def _():
            for r in starts:
                k = r - lo
                ex, ey, ez = (left_e[t, c, k:k + 8, :] for c in range(3))
                ex_z = left_e[t, 0, k + 1:k + 9, :]
                ey_x, ez_x = (f[c, 0, r:r + 8, :] for c in (1, 2))
                left_h[0, k:k + 8, :] -= DT * ((ex_z - ex) - (ez_x - ez))
                left_h[1, k:k + 8, :] -= DT * ((ey_x - ey) - (y_up(ex) - ex))

        h_plane(last - 1, next_plane(last - 1))
        h_plane(last, lambda c, r: right_e[t, c, r - lo:r - lo + 8, :])
        e_plane(last, previous_plane(last))

        @pl.when(t < TOTAL - 1)
        def _():
            start_right(t + 1)
        done(t, last)

        h_plane(0, next_plane(0))
        e_plane(0, lambda c, r: left_h[c, r - lo:r - lo + 8, :])

        @pl.when(t < TOTAL - 1)
        def _():
            start_left(t + 1)
        done(t, 0)

        def inner(x, c):
            h_plane(x, next_plane(x))
            e_plane(x, previous_plane(x))
            done(t, x)
            return c
        lax.fori_loop(1, last - 1, inner, 0)
        e_plane(last - 1, previous_plane(last - 1))
        done(t, last - 1)
        return carry

    lax.fori_loop(0, TOTAL, step, 0)

    @pl.when(jnp.logical_not(has_up))
    def _():
        def body(x, carry):
            got[:, x, 0:HALO, :] = f[:, x, end:hi, :]
            return carry
        lax.fori_loop(0, nx, body, 0)

    outs = (e_out, h_out, p_out)

    def leave(x):
        return [pltpu.make_async_copy(made.at[3 * k:3 * k + 3, x], outs[k].at[:, x], out_sem.at[k, x]) for k in range(3)]

    def assemble(n, carry):
        x = jnp.where(n == 0, last, n - 1)

        @pl.when(has_up)
        def _():
            final(x).wait_recv()
        for c in range(9):
            joined[c, 0:SMAX, :] = f[c, x, end - SMAX:end, :]
            joined[c, SMAX:SMAX + rows_sent, :] = got[c, x, 0:rows_sent, :]
        for c in range(9):
            for k in range(0, nz, 8):
                made[c, x, k:k + 8, :] = joined[c, pl.ds(total + (SMAX - nz) + k, 8), :]
        for copy in leave(x):
            copy.start()
        return carry

    lax.fori_loop(0, nx, assemble, 0)

    def finish(x, carry):
        for copy in leave(x):
            copy.wait()

        @pl.when(has_dn)
        def _():
            final(x).wait_send()
        return carry
    lax.fori_loop(0, nx, finish, 0)


def run(rows_sent, collective, e_field, h_field, polar, polar_rate, material, shift_counts):
    nx, nz, ny = material.shape
    span = nz + 2 * HALO
    tall = span + 2 * PAD
    f32 = jnp.float32
    dma = pltpu.SemaphoreType.DMA
    anywhere = pl.BlockSpec(memory_space=pl.ANY)
    return pl.pallas_call(
        functools.partial(kernel, rows_sent),
        out_shape=[jax.ShapeDtypeStruct(e_field.shape, f32)] * 3,
        in_specs=[anywhere] * 5 + [pl.BlockSpec(memory_space=pltpu.SMEM)],
        out_specs=[anywhere] * 3,
        scratch_shapes=[
            pltpu.VMEM((9, nx, tall, ny), f32),
            pltpu.VMEM((3, nx, tall, ny), f32),
            pltpu.VMEM((9, nx, nz, ny), f32),
            pltpu.VMEM((9, SMAX + nz, ny), f32),
            pltpu.VMEM((9, nx, nz, ny), f32),
            pltpu.VMEM((nx, tall, ny), jnp.int32),
            pltpu.VMEM((nx, BELOW + nz + HALO, ny), jnp.int32),
            pltpu.VMEM((nx, SMAX, ny), jnp.int32),
            pltpu.VMEM((TOTAL, 3, span + PAD, ny), f32),
            pltpu.VMEM((TOTAL, 2, span, ny), f32),
            pltpu.VMEM((2, span, ny), f32),
            pltpu.VMEM((2, tall, ny), f32),
            dma((5,)), dma((2, 5)), dma((2, 5)),
            dma((TOTAL,)), dma((TOTAL,)), dma((TOTAL,)), dma((TOTAL,)),
            dma, dma, dma, dma,
            dma((nx,)), dma((nx,)), dma((3, nx)),
        ],
        compiler_params=pltpu.CompilerParams(
            collective_id=collective, has_side_effects=True, vmem_limit_bytes=52 * 1024 * 1024),
    )(e_field, h_field, polar, polar_rate, material, shift_counts)


def local(e_field, h_field, polar, polar_rate, material, shift_counts):
    counts = list(range(SMAX + 8, CYCLES * SMAX + 1, 8))
    chosen = jnp.clip((shift_counts[0] + shift_counts[1] + 7) // 8 - counts[0] // 8, 0, len(counts) - 1)
    branches = [functools.partial(run, rows, k) for k, rows in enumerate(counts)]
    return tuple(lax.switch(chosen, branches, e_field, h_field, polar, polar_rate, material, shift_counts))


def solution(mesh):
    placed = (
        P(None, "ta", "gz", None),
        P(None, "ta", "gz", None),
        P(None, "ta", "gz", None),
        P(None, "ta", "gz", None),
        P("ta", "gz", None),
        P(),
    )
    return jax.shard_map(
        local,
        mesh=mesh,
        in_specs=placed,
        out_specs=(P(None, "ta", "gz", None), P(None, "ta", "gz", None), P(None, "ta", "gz", None)),
        check_vma=False,
    )
```

```python
import functools

import jax
import jax.numpy as jnp
from jax import lax
from jax.experimental import pallas as pl
from jax.experimental.pallas import tpu as pltpu
from jax.sharding import PartitionSpec as P

SMAX = 32
STEPS = 4
CYCLES = 2
TOTAL = STEPS * CYCLES
HALO = 8
PAD = 8
BELOW = SMAX + HALO
OWN = PAD + HALO
DT = 0.5
MESH = pl.DeviceIdType.MESH


def kernel(rows_sent, e_in, h_in, p_in, q_in, m_in, counts, e_out, h_out, p_out,
           f, q, got, joined, made, mat, own_mat, late_mat, left_e, right_e, left_h, masks,
           load_sem, zs_sem, zr_sem, xls, xlr, xrs, xrr, hs, hr, ms, mr, fs, fr, out_sem):
    nx, nz, ny = m_in.shape
    end = OWN + nz
    lo, hi = PAD, end + HALO
    span = hi - lo
    gz, ta = lax.axis_index("gz"), lax.axis_index("ta")
    ngz, nta = lax.axis_size("gz"), lax.axis_size("ta")
    has_dn, has_up = gz > 0, gz < ngz - 1
    has_l, has_r = ta > 0, ta < nta - 1
    dn, up = {"gz": gz - 1}, {"gz": gz + 1}
    lt, rt = {"ta": ta - 1}, {"ta": ta + 1}
    s0, s1 = jnp.clip(counts[0], 1, SMAX), jnp.clip(counts[1], 1, SMAX)
    total = jnp.clip(s0 + s1, SMAX, CYCLES * SMAX)

    loads = [
        pltpu.make_async_copy(e_in, f.at[0:3, :, OWN:end, :], load_sem.at[0]),
        pltpu.make_async_copy(h_in, f.at[3:6, :, OWN:end, :], load_sem.at[1]),
        pltpu.make_async_copy(p_in, f.at[6:9, :, OWN:end, :], load_sem.at[2]),
        pltpu.make_async_copy(q_in, q.at[:, :, OWN:end, :], load_sem.at[3]),
        pltpu.make_async_copy(m_in, own_mat.at[:, BELOW:BELOW + nz, :], load_sem.at[4]),
    ]
    for copy in loads:
        copy.start()

    barrier = pltpu.get_barrier_semaphore()
    around = ((has_dn, dn), (has_up, up), (has_l, lt), (has_r, rt))
    for there, device in around:
        @pl.when(there)
        def _():
            pl.semaphore_signal(barrier, inc=1, device_id=device, device_id_type=MESH)
    pl.semaphore_wait(barrier, sum(there.astype(jnp.int32) for there, _ in around))

    def remote(src, dst, send, recv, device):
        return pltpu.make_async_remote_copy(src_ref=src, dst_ref=dst, send_sem=send, recv_sem=recv,
                                            device_id=device, device_id_type=MESH)

    down, upward = [], []
    for k, (src, dst) in enumerate(((e_in, f.at[0:3]), (h_in, f.at[3:6]), (p_in, f.at[6:9]), (q_in, q))):
        down.append(remote(src.at[:, :, 0:HALO, :], dst.at[:, :, end:hi, :], zs_sem.at[0, k], zr_sem.at[0, k], dn))
        upward.append(remote(src.at[:, :, nz - HALO:nz, :], dst.at[:, :, lo:OWN, :], zs_sem.at[1, k], zr_sem.at[1, k], up))
    down.append(remote(m_in.at[:, 0:HALO, :], own_mat.at[:, BELOW + nz:BELOW + nz + HALO, :], zs_sem.at[0, 4], zr_sem.at[0, 4], dn))
    upward.append(remote(m_in.at[:, nz - HALO:nz, :], own_mat.at[:, SMAX:BELOW, :], zs_sem.at[1, 4], zr_sem.at[1, 4], up))
    later = remote(m_in.at[:, nz - BELOW:nz - HALO, :], late_mat, ms, mr, up)

    @pl.when(has_dn)
    def _():
        for copy in down:
            copy.start()

    @pl.when(has_up)
    def _():
        for copy in upward:
            copy.start()
        later.start()

    def edge_rows(first, last):
        def body(x, carry):
            f[:, x, first:last, :] = jnp.zeros((9, last - first, ny), jnp.float32)
            q[:, x, first:last, :] = jnp.zeros((3, last - first, ny), jnp.float32)
            return carry
        lax.fori_loop(0, nx, body, 0)

    edge_rows(0, lo)
    edge_rows(hi, hi + PAD)

    @pl.when(jnp.logical_not(has_dn))
    def _():
        edge_rows(lo, OWN)
        def body(x, carry):
            own_mat[x, 0:BELOW, :] = jnp.zeros((BELOW, ny), jnp.int32)
            late_mat[x] = jnp.zeros((SMAX, ny), jnp.int32)
            return carry
        lax.fori_loop(0, nx, body, 0)

    @pl.when(jnp.logical_not(has_up))
    def _():
        edge_rows(end, hi)
        def body(x, carry):
            own_mat[x, BELOW + nz:BELOW + nz + HALO, :] = jnp.zeros((HALO, ny), jnp.int32)
            got[:, x] = jnp.zeros(got.at[:, x].shape, jnp.float32)
            return carry
        lax.fori_loop(0, nx, body, 0)

    def clear_slot(t, carry):
        left_e[t, :, span:span + PAD, :] = jnp.zeros((3, PAD, ny), jnp.float32)

        @pl.when(jnp.logical_not(has_l))
        def _():
            left_e[t, :, 0:span, :] = jnp.zeros((3, span, ny), jnp.float32)

        @pl.when(jnp.logical_not(has_r))
        def _():
            right_e[t] = jnp.zeros((2, span, ny), jnp.float32)
        return carry
    lax.fori_loop(0, TOTAL, clear_slot, 0)

    @pl.when(jnp.logical_not(has_l))
    def _():
        left_h[...] = jnp.zeros(left_h.shape, jnp.float32)

    for copy in loads:
        copy.wait()

    @pl.when(has_dn)
    def _():
        for copy in down:
            copy.wait_send()
        for copy in upward:
            copy.wait_recv()

    @pl.when(has_up)
    def _():
        for copy in upward:
            copy.wait_send()
        for copy in down:
            copy.wait_recv()

    def to_left(t):
        return remote(f.at[1:3, 0, lo:hi, :], right_e.at[t], xls.at[t], xlr.at[t], lt)

    def to_right(t):
        return remote(f.at[0:3, nx - 1, lo:hi, :], left_e.at[t, :, 0:span, :], xrs.at[t], xrr.at[t], rt)

    first_h = remote(f.at[4:6, nx - 1, lo:hi, :], left_h, hs, hr, rt)

    def start_left(t):
        @pl.when(has_l)
        def _():
            to_left(t).start()

    def start_right(t):
        @pl.when(has_r)
        def _():
            to_right(t).start()

    def wait_x(t):
        @pl.when(has_l)
        def _():
            to_left(t).wait_send()
            to_right(t).wait_recv()

        @pl.when(has_r)
        def _():
            to_right(t).wait_send()
            to_left(t).wait_recv()

    start_left(0)
    start_right(0)

    @pl.when(has_r)
    def _():
        first_h.start()
        first_h.wait_send()

    @pl.when(has_l)
    def _():
        first_h.wait_recv()

    lane = lax.broadcasted_iota(jnp.int32, (8, ny), 1)
    row = lax.broadcasted_iota(jnp.int32, (8, ny), 0)
    starts = list(range(lo, hi, 8))

    def y_up(v):
        return jnp.where(lane < ny - 1, pltpu.roll(v, ny - 1, 1), 0.0)

    def y_down(v):
        return jnp.where(lane > 0, pltpu.roll(v, 1, 1), 0.0)

    def new_cycle(shift):
        low = shift
        high = ngz * nz + shift
        for r in starts:
            place = gz * nz + (r - OWN) + row
            masks[0, r:r + 8, :] = jnp.where(place - 1 >= low, 1.0, 0.0)
            masks[1, r:r + 8, :] = jnp.where(place < high, DT, 0.0)

        def body(x, carry):
            for r in starts:
                mat[x, r:r + 8, :] = own_mat[x, pl.ds(SMAX - shift + (r - lo), 8), :]
            return carry
        lax.fori_loop(0, nx, body, 0)

    def h_rows(x, after, r):
        ex, ey, ez = (f[c, x, r:r + 8, :] for c in range(3))
        ex_z, ey_z = (f[c, x, r + 1:r + 9, :] for c in range(2))
        ey_x, ez_x = after(0, r), after(1, r)
        old = [f[3 + c, x, r:r + 8, :] for c in range(3)]
        curl = (
            (y_up(ez) - ez) - (ey_z - ey),
            (ex_z - ex) - (ez_x - ez),
            (ey_x - ey) - (y_up(ex) - ex),
        )

        def store():
            for c in range(3):
                f[3 + c, x, r:r + 8, :] = old[c] - DT * curl[c]
        return store

    def next_plane(x):
        return lambda c, r: f[1 + c, x + 1, r:r + 8, :]

    def e_rows(x, before, r):
        hx, hy, hz = (f[3 + c, x, r:r + 8, :] for c in range(3))
        keep = masks[0, r:r + 8, :]
        hx_z = f[3, x, r - 1:r + 7, :] * keep
        hy_z = f[4, x, r - 1:r + 7, :] * keep
        hy_x, hz_x = before(0, r), before(1, r)
        curl = (
            (hz - y_down(hz)) - (hy - hy_z),
            (hx - hx_z) - (hz - hz_x),
            (hy - hy_x) - (hx - y_down(hx)),
        )
        core = mat[x, r:r + 8, :] == 1
        keep_rate = jnp.where(core, 1.0 - DT * 0.05, 1.0 - DT * 0.2)
        drive = jnp.where(core, DT * 1.44 * 0.5, DT * 4.0 * 0.2)
        spring = jnp.where(core, DT * 1.44, DT * 4.0)
        eps = jnp.where(core, 11.7, 2.1)
        bend = jnp.where(core, 11.7 * 0.05, 2.1 * 0.01)
        e = [f[c, x, r:r + 8, :] for c in range(3)]
        intensity = e[0] * e[0] + e[1] * e[1] + e[2] * e[2]
        gain = masks[1, r:r + 8, :] / (eps + bend * intensity)
        p = [f[6 + c, x, r:r + 8, :] for c in range(3)]
        rate = [keep_rate * q[c, x, r:r + 8, :] + (drive * e[c] - spring * p[c]) for c in range(3)]

        def store():
            for c in range(3):
                q[c, x, r:r + 8, :] = rate[c]
                f[6 + c, x, r:r + 8, :] = p[c] + DT * rate[c]
                f[c, x, r:r + 8, :] = e[c] + gain * (curl[c] - rate[c])
        return store

    def sweep(*works):
        for n in range(0, len(starts), 2):
            stores = [work(r) for r in starts[n:n + 2] for work in works]
            for store in stores:
                store()

    def h_plane(x, after):
        return lambda r: h_rows(x, after, r)

    def e_plane(x, before):
        return lambda r: e_rows(x, before, r)

    def previous_plane(x):
        return lambda c, r: f[4 + c, x - 1, r:r + 8, :]

    def final(x):
        return remote(f.at[:, x, OWN:OWN + rows_sent, :], got.at[:, x, 0:rows_sent, :], fs.at[x], fr.at[x], dn)

    def done(t, x):
        @pl.when(jnp.logical_and(t == TOTAL - 1, has_dn))
        def _():
            final(x).start()

    last = nx - 1

    def step(t, carry):
        @pl.when(t == 0)
        def _():
            new_cycle(jnp.int32(0))

        @pl.when(t == STEPS)
        def _():
            @pl.when(has_up)
            def _():
                later.wait_send()

            @pl.when(has_dn)
            def _():
                later.wait_recv()

            def body(x, c):
                own_mat[x, 0:SMAX, :] = late_mat[x]
                return c
            lax.fori_loop(0, nx, body, 0)
            new_cycle(s0)

        wait_x(t)

        @pl.when(has_l)
        def _():
            for r in starts:
                k = r - lo
                ex, ey, ez = (left_e[t, c, k:k + 8, :] for c in range(3))
                ex_z = left_e[t, 0, k + 1:k + 9, :]
                ey_x, ez_x = (f[c, 0, r:r + 8, :] for c in (1, 2))
                left_h[0, k:k + 8, :] -= DT * ((ex_z - ex) - (ez_x - ez))
                left_h[1, k:k + 8, :] -= DT * ((ey_x - ey) - (y_up(ex) - ex))

        sweep(h_plane(last - 1, next_plane(last - 1)),
              h_plane(last, lambda c, r: right_e[t, c, r - lo:r - lo + 8, :]))
        sweep(h_plane(0, next_plane(0)), e_plane(last, previous_plane(last)))

        @pl.when(t < TOTAL - 1)
        def _():
            start_right(t + 1)
        done(t, last)

        sweep(h_plane(1, next_plane(1)), e_plane(0, lambda c, r: left_h[c, r - lo:r - lo + 8, :]))

        @pl.when(t < TOTAL - 1)
        def _():
            start_left(t + 1)
        done(t, 0)

        def inner(x, c):
            sweep(h_plane(x + 1, next_plane(x + 1)), e_plane(x, previous_plane(x)))
            done(t, x)
            return c
        lax.fori_loop(1, last - 2, inner, 0)
        sweep(e_plane(last - 2, previous_plane(last - 2)))
        done(t, last - 2)
        sweep(e_plane(last - 1, previous_plane(last - 1)))
        done(t, last - 1)
        return carry

    lax.fori_loop(0, TOTAL, step, 0)

    @pl.when(jnp.logical_not(has_up))
    def _():
        def body(x, carry):
            got[:, x, 0:HALO, :] = f[:, x, end:hi, :]
            return carry
        lax.fori_loop(0, nx, body, 0)

    outs = (e_out, h_out, p_out)

    def leave(x):
        return [pltpu.make_async_copy(made.at[3 * k:3 * k + 3, x], outs[k].at[:, x], out_sem.at[k, x]) for k in range(3)]

    def assemble(n, carry):
        x = jnp.where(n == 0, last, n - 1)

        @pl.when(has_up)
        def _():
            final(x).wait_recv()
        for c in range(9):
            joined[c, 0:SMAX, :] = f[c, x, end - SMAX:end, :]
            joined[c, SMAX:SMAX + rows_sent, :] = got[c, x, 0:rows_sent, :]
        for c in range(9):
            for k in range(0, nz, 8):
                made[c, x, k:k + 8, :] = joined[c, pl.ds(total + (SMAX - nz) + k, 8), :]
        for copy in leave(x):
            copy.start()
        return carry

    lax.fori_loop(0, nx, assemble, 0)

    def finish(x, carry):
        for copy in leave(x):
            copy.wait()

        @pl.when(has_dn)
        def _():
            final(x).wait_send()
        return carry
    lax.fori_loop(0, nx, finish, 0)


def run(rows_sent, collective, e_field, h_field, polar, polar_rate, material, shift_counts):
    nx, nz, ny = material.shape
    span = nz + 2 * HALO
    tall = span + 2 * PAD
    f32 = jnp.float32
    dma = pltpu.SemaphoreType.DMA
    anywhere = pl.BlockSpec(memory_space=pl.ANY)
    return pl.pallas_call(
        functools.partial(kernel, rows_sent),
        out_shape=[jax.ShapeDtypeStruct(e_field.shape, f32)] * 3,
        in_specs=[anywhere] * 5 + [pl.BlockSpec(memory_space=pltpu.SMEM)],
        out_specs=[anywhere] * 3,
        scratch_shapes=[
            pltpu.VMEM((9, nx, tall, ny), f32),
            pltpu.VMEM((3, nx, tall, ny), f32),
            pltpu.VMEM((9, nx, nz, ny), f32),
            pltpu.VMEM((9, SMAX + nz, ny), f32),
            pltpu.VMEM((9, nx, nz, ny), f32),
            pltpu.VMEM((nx, tall, ny), jnp.int32),
            pltpu.VMEM((nx, BELOW + nz + HALO, ny), jnp.int32),
            pltpu.VMEM((nx, SMAX, ny), jnp.int32),
            pltpu.VMEM((TOTAL, 3, span + PAD, ny), f32),
            pltpu.VMEM((TOTAL, 2, span, ny), f32),
            pltpu.VMEM((2, span, ny), f32),
            pltpu.VMEM((2, tall, ny), f32),
            dma((5,)), dma((2, 5)), dma((2, 5)),
            dma((TOTAL,)), dma((TOTAL,)), dma((TOTAL,)), dma((TOTAL,)),
            dma, dma, dma, dma,
            dma((nx,)), dma((nx,)), dma((3, nx)),
        ],
        compiler_params=pltpu.CompilerParams(
            collective_id=collective, has_side_effects=True, vmem_limit_bytes=52 * 1024 * 1024),
    )(e_field, h_field, polar, polar_rate, material, shift_counts)


def local(e_field, h_field, polar, polar_rate, material, shift_counts):
    counts = list(range(SMAX + 8, CYCLES * SMAX + 1, 8))
    chosen = jnp.clip((shift_counts[0] + shift_counts[1] + 7) // 8 - counts[0] // 8, 0, len(counts) - 1)
    branches = [functools.partial(run, rows, k) for k, rows in enumerate(counts)]
    return tuple(lax.switch(chosen, branches, e_field, h_field, polar, polar_rate, material, shift_counts))


def solution(mesh):
    placed = (
        P(None, "ta", "gz", None),
        P(None, "ta", "gz", None),
        P(None, "ta", "gz", None),
        P(None, "ta", "gz", None),
        P("ta", "gz", None),
        P(),
    )
    return jax.shard_map(
        local,
        mesh=mesh,
        in_specs=placed,
        out_specs=(P(None, "ta", "gz", None), P(None, "ta", "gz", None), P(None, "ta", "gz", None)),
        check_vma=False,
    )
```

```python
import functools

import jax
import jax.numpy as jnp
from jax import lax
from jax.experimental import pallas as pl
from jax.experimental.pallas import tpu as pltpu
from jax.sharding import PartitionSpec as P

SMAX = 32
STEPS = 4
CYCLES = 2
TOTAL = STEPS * CYCLES
HALO = 8
PAD = 8
BELOW = SMAX + HALO
OWN = PAD + HALO
DT = 0.5
MESH = pl.DeviceIdType.MESH


def kernel(rows_sent, e_in, h_in, p_in, q_in, m_in, counts, e_out, h_out, p_out,
           f, q, got, joined, made, mat, own_mat, late_mat, left_e, right_e, left_h, masks,
           load_sem, zs_sem, zr_sem, xls, xlr, xrs, xrr, hs, hr, ms, mr, fs, fr, out_sem):
    nx, nz, ny = m_in.shape
    end = OWN + nz
    lo, hi = PAD, end + HALO
    span = hi - lo
    gz, ta = lax.axis_index("gz"), lax.axis_index("ta")
    ngz, nta = lax.axis_size("gz"), lax.axis_size("ta")
    has_dn, has_up = gz > 0, gz < ngz - 1
    has_l, has_r = ta > 0, ta < nta - 1
    dn, up = {"gz": gz - 1}, {"gz": gz + 1}
    lt, rt = {"ta": ta - 1}, {"ta": ta + 1}
    s0, s1 = jnp.clip(counts[0], 1, SMAX), jnp.clip(counts[1], 1, SMAX)
    total = jnp.clip(s0 + s1, SMAX, CYCLES * SMAX)

    loads = [
        pltpu.make_async_copy(e_in, f.at[0:3, :, OWN:end, :], load_sem.at[0]),
        pltpu.make_async_copy(h_in, f.at[3:6, :, OWN:end, :], load_sem.at[1]),
        pltpu.make_async_copy(p_in, f.at[6:9, :, OWN:end, :], load_sem.at[2]),
        pltpu.make_async_copy(q_in, q.at[:, :, OWN:end, :], load_sem.at[3]),
        pltpu.make_async_copy(m_in, own_mat.at[:, BELOW:BELOW + nz, :], load_sem.at[4]),
    ]
    for copy in loads:
        copy.start()

    barrier = pltpu.get_barrier_semaphore()
    around = ((has_dn, dn), (has_up, up), (has_l, lt), (has_r, rt))
    for there, device in around:
        @pl.when(there)
        def _():
            pl.semaphore_signal(barrier, inc=1, device_id=device, device_id_type=MESH)
    pl.semaphore_wait(barrier, sum(there.astype(jnp.int32) for there, _ in around))

    def remote(src, dst, send, recv, device):
        return pltpu.make_async_remote_copy(src_ref=src, dst_ref=dst, send_sem=send, recv_sem=recv,
                                            device_id=device, device_id_type=MESH)

    down, upward = [], []
    for k, (src, dst) in enumerate(((e_in, f.at[0:3]), (h_in, f.at[3:6]), (p_in, f.at[6:9]), (q_in, q))):
        down.append(remote(src.at[:, :, 0:HALO, :], dst.at[:, :, end:hi, :], zs_sem.at[0, k], zr_sem.at[0, k], dn))
        upward.append(remote(src.at[:, :, nz - HALO:nz, :], dst.at[:, :, lo:OWN, :], zs_sem.at[1, k], zr_sem.at[1, k], up))
    down.append(remote(m_in.at[:, 0:HALO, :], own_mat.at[:, BELOW + nz:BELOW + nz + HALO, :], zs_sem.at[0, 4], zr_sem.at[0, 4], dn))
    upward.append(remote(m_in.at[:, nz - HALO:nz, :], own_mat.at[:, SMAX:BELOW, :], zs_sem.at[1, 4], zr_sem.at[1, 4], up))
    later = remote(m_in.at[:, nz - BELOW:nz - HALO, :], late_mat, ms, mr, up)

    @pl.when(has_dn)
    def _():
        for copy in down:
            copy.start()

    @pl.when(has_up)
    def _():
        for copy in upward:
            copy.start()

    def edge_rows(first, last):
        def body(x, carry):
            f[:, x, first:last, :] = jnp.zeros((9, last - first, ny), jnp.float32)
            q[:, x, first:last, :] = jnp.zeros((3, last - first, ny), jnp.float32)
            return carry
        lax.fori_loop(0, nx, body, 0)

    edge_rows(0, lo)
    edge_rows(hi, hi + PAD)

    @pl.when(jnp.logical_not(has_dn))
    def _():
        edge_rows(lo, OWN)
        def body(x, carry):
            own_mat[x, 0:BELOW, :] = jnp.zeros((BELOW, ny), jnp.int32)
            late_mat[x] = jnp.zeros((SMAX, ny), jnp.int32)
            return carry
        lax.fori_loop(0, nx, body, 0)

    @pl.when(jnp.logical_not(has_up))
    def _():
        edge_rows(end, hi)
        def body(x, carry):
            own_mat[x, BELOW + nz:BELOW + nz + HALO, :] = jnp.zeros((HALO, ny), jnp.int32)
            got[:, x] = jnp.zeros(got.at[:, x].shape, jnp.float32)
            return carry
        lax.fori_loop(0, nx, body, 0)

    def clear_slot(t, carry):
        left_e[t, :, span:span + PAD, :] = jnp.zeros((3, PAD, ny), jnp.float32)

        @pl.when(jnp.logical_not(has_l))
        def _():
            left_e[t, :, 0:span, :] = jnp.zeros((3, span, ny), jnp.float32)

        @pl.when(jnp.logical_not(has_r))
        def _():
            right_e[t] = jnp.zeros((2, span, ny), jnp.float32)
        return carry
    lax.fori_loop(0, TOTAL, clear_slot, 0)

    @pl.when(jnp.logical_not(has_l))
    def _():
        left_h[...] = jnp.zeros(left_h.shape, jnp.float32)

    for copy in loads:
        copy.wait()

    @pl.when(has_dn)
    def _():
        for copy in down:
            copy.wait_send()
        for copy in upward:
            copy.wait_recv()

    @pl.when(has_up)
    def _():
        for copy in upward:
            copy.wait_send()
        for copy in down:
            copy.wait_recv()

    def to_left(t):
        return remote(f.at[1:3, 0, lo:hi, :], right_e.at[t], xls.at[t], xlr.at[t], lt)

    def to_right(t):
        return remote(f.at[0:3, nx - 1, lo:hi, :], left_e.at[t, :, 0:span, :], xrs.at[t], xrr.at[t], rt)

    first_h = remote(f.at[4:6, nx - 1, lo:hi, :], left_h, hs, hr, rt)

    def start_left(t):
        @pl.when(has_l)
        def _():
            to_left(t).start()

    def start_right(t):
        @pl.when(has_r)
        def _():
            to_right(t).start()

    def wait_x(t):
        @pl.when(has_l)
        def _():
            to_left(t).wait_send()
            to_right(t).wait_recv()

        @pl.when(has_r)
        def _():
            to_right(t).wait_send()
            to_left(t).wait_recv()

    @pl.when(has_r)
    def _():
        first_h.start()

    start_left(0)
    start_right(0)

    @pl.when(has_up)
    def _():
        later.start()

    lane = lax.broadcasted_iota(jnp.int32, (8, ny), 1)
    row = lax.broadcasted_iota(jnp.int32, (8, ny), 0)
    starts = list(range(lo, hi, 8))

    def y_up(v):
        return jnp.where(lane < ny - 1, pltpu.roll(v, ny - 1, 1), 0.0)

    def y_down(v):
        return jnp.where(lane > 0, pltpu.roll(v, 1, 1), 0.0)

    def new_cycle(shift):
        low = shift
        high = ngz * nz + shift
        for r in starts:
            place = gz * nz + (r - OWN) + row
            masks[0, r:r + 8, :] = jnp.where(place - 1 >= low, 1.0, 0.0)
            masks[1, r:r + 8, :] = jnp.where(place < high, DT, 0.0)

        def body(x, carry):
            for r in starts:
                mat[x, r:r + 8, :] = own_mat[x, pl.ds(SMAX - shift + (r - lo), 8), :]
            return carry
        lax.fori_loop(0, nx, body, 0)

    def h_rows(x, after, r):
        ex, ey, ez = (f[c, x, r:r + 8, :] for c in range(3))
        ex_z, ey_z = (f[c, x, r + 1:r + 9, :] for c in range(2))
        ey_x, ez_x = after(0, r), after(1, r)
        old = [f[3 + c, x, r:r + 8, :] for c in range(3)]
        curl = (
            (y_up(ez) - ez) - (ey_z - ey),
            (ex_z - ex) - (ez_x - ez),
            (ey_x - ey) - (y_up(ex) - ex),
        )

        def store():
            for c in range(3):
                f[3 + c, x, r:r + 8, :] = old[c] - DT * curl[c]
        return store

    def next_plane(x):
        return lambda c, r: f[1 + c, x + 1, r:r + 8, :]

    def e_rows(x, before, r):
        hx, hy, hz = (f[3 + c, x, r:r + 8, :] for c in range(3))
        keep = masks[0, r:r + 8, :]
        hx_z = f[3, x, r - 1:r + 7, :] * keep
        hy_z = f[4, x, r - 1:r + 7, :] * keep
        hy_x, hz_x = before(0, r), before(1, r)
        curl = (
            (hz - y_down(hz)) - (hy - hy_z),
            (hx - hx_z) - (hz - hz_x),
            (hy - hy_x) - (hx - y_down(hx)),
        )
        core = mat[x, r:r + 8, :] == 1
        keep_rate = jnp.where(core, 1.0 - DT * 0.05, 1.0 - DT * 0.2)
        drive = jnp.where(core, DT * 1.44 * 0.5, DT * 4.0 * 0.2)
        spring = jnp.where(core, DT * 1.44, DT * 4.0)
        eps = jnp.where(core, 11.7, 2.1)
        bend = jnp.where(core, 11.7 * 0.05, 2.1 * 0.01)
        e = [f[c, x, r:r + 8, :] for c in range(3)]
        intensity = e[0] * e[0] + e[1] * e[1] + e[2] * e[2]
        gain = masks[1, r:r + 8, :] / (eps + bend * intensity)
        p = [f[6 + c, x, r:r + 8, :] for c in range(3)]
        rate = [keep_rate * q[c, x, r:r + 8, :] + (drive * e[c] - spring * p[c]) for c in range(3)]

        def store():
            for c in range(3):
                q[c, x, r:r + 8, :] = rate[c]
                f[6 + c, x, r:r + 8, :] = p[c] + DT * rate[c]
                f[c, x, r:r + 8, :] = e[c] + gain * (curl[c] - rate[c])
        return store

    def sweep(*works):
        for n in range(0, len(starts), 2):
            stores = [work(r) for r in starts[n:n + 2] for work in works]
            for store in stores:
                store()

    def h_plane(x, after):
        return lambda r: h_rows(x, after, r)

    def e_plane(x, before):
        return lambda r: e_rows(x, before, r)

    def previous_plane(x):
        return lambda c, r: f[4 + c, x - 1, r:r + 8, :]

    def final(x):
        return remote(f.at[:, x, OWN:OWN + rows_sent, :], got.at[:, x, 0:rows_sent, :], fs.at[x], fr.at[x], dn)

    def done(t, x):
        @pl.when(jnp.logical_and(t == TOTAL - 1, has_dn))
        def _():
            final(x).start()

    last = nx - 1

    def step(t, carry):
        @pl.when(t == 0)
        def _():
            new_cycle(jnp.int32(0))

            @pl.when(has_r)
            def _():
                first_h.wait_send()

            @pl.when(has_l)
            def _():
                first_h.wait_recv()

        @pl.when(t == STEPS)
        def _():
            @pl.when(has_up)
            def _():
                later.wait_send()

            @pl.when(has_dn)
            def _():
                later.wait_recv()

            def body(x, c):
                own_mat[x, 0:SMAX, :] = late_mat[x]
                return c
            lax.fori_loop(0, nx, body, 0)
            new_cycle(s0)

        wait_x(t)

        @pl.when(has_l)
        def _():
            for r in starts:
                k = r - lo
                ex, ey, ez = (left_e[t, c, k:k + 8, :] for c in range(3))
                ex_z = left_e[t, 0, k + 1:k + 9, :]
                ey_x, ez_x = (f[c, 0, r:r + 8, :] for c in (1, 2))
                left_h[0, k:k + 8, :] -= DT * ((ex_z - ex) - (ez_x - ez))
                left_h[1, k:k + 8, :] -= DT * ((ey_x - ey) - (y_up(ex) - ex))

        sweep(h_plane(last - 1, next_plane(last - 1)),
              h_plane(last, lambda c, r: right_e[t, c, r - lo:r - lo + 8, :]))
        sweep(h_plane(0, next_plane(0)), e_plane(last, previous_plane(last)))

        @pl.when(t < TOTAL - 1)
        def _():
            start_right(t + 1)
        done(t, last)

        sweep(h_plane(1, next_plane(1)), e_plane(0, lambda c, r: left_h[c, r - lo:r - lo + 8, :]))

        @pl.when(t < TOTAL - 1)
        def _():
            start_left(t + 1)
        done(t, 0)

        def inner(x, c):
            sweep(h_plane(x + 1, next_plane(x + 1)), e_plane(x, previous_plane(x)))
            done(t, x)
            return c
        lax.fori_loop(1, last - 2, inner, 0)
        sweep(e_plane(last - 2, previous_plane(last - 2)))
        done(t, last - 2)
        sweep(e_plane(last - 1, previous_plane(last - 1)))
        done(t, last - 1)
        return carry

    lax.fori_loop(0, TOTAL, step, 0)

    @pl.when(jnp.logical_not(has_up))
    def _():
        def body(x, carry):
            got[:, x, 0:HALO, :] = f[:, x, end:hi, :]
            return carry
        lax.fori_loop(0, nx, body, 0)

    outs = (e_out, h_out, p_out)

    def leave(x):
        return [pltpu.make_async_copy(made.at[3 * k:3 * k + 3, x], outs[k].at[:, x], out_sem.at[k, x]) for k in range(3)]

    def assemble(n, carry):
        x = jnp.where(n == 0, last, n - 1)

        @pl.when(has_up)
        def _():
            final(x).wait_recv()
        for c in range(9):
            joined[c, 0:SMAX, :] = f[c, x, end - SMAX:end, :]
            joined[c, SMAX:SMAX + rows_sent, :] = got[c, x, 0:rows_sent, :]
        for c in range(9):
            for k in range(0, nz, 8):
                made[c, x, k:k + 8, :] = joined[c, pl.ds(total + (SMAX - nz) + k, 8), :]
        for copy in leave(x):
            copy.start()
        return carry

    lax.fori_loop(0, nx, assemble, 0)

    def finish(x, carry):
        for copy in leave(x):
            copy.wait()

        @pl.when(has_dn)
        def _():
            final(x).wait_send()
        return carry
    lax.fori_loop(0, nx, finish, 0)


def run(rows_sent, collective, e_field, h_field, polar, polar_rate, material, shift_counts):
    nx, nz, ny = material.shape
    span = nz + 2 * HALO
    tall = span + 2 * PAD
    f32 = jnp.float32
    dma = pltpu.SemaphoreType.DMA
    anywhere = pl.BlockSpec(memory_space=pl.ANY)
    return pl.pallas_call(
        functools.partial(kernel, rows_sent),
        out_shape=[jax.ShapeDtypeStruct(e_field.shape, f32)] * 3,
        in_specs=[anywhere] * 5 + [pl.BlockSpec(memory_space=pltpu.SMEM)],
        out_specs=[anywhere] * 3,
        scratch_shapes=[
            pltpu.VMEM((9, nx, tall, ny), f32),
            pltpu.VMEM((3, nx, tall, ny), f32),
            pltpu.VMEM((9, nx, nz, ny), f32),
            pltpu.VMEM((9, SMAX + nz, ny), f32),
            pltpu.VMEM((9, nx, nz, ny), f32),
            pltpu.VMEM((nx, tall, ny), jnp.int32),
            pltpu.VMEM((nx, BELOW + nz + HALO, ny), jnp.int32),
            pltpu.VMEM((nx, SMAX, ny), jnp.int32),
            pltpu.VMEM((TOTAL, 3, span + PAD, ny), f32),
            pltpu.VMEM((TOTAL, 2, span, ny), f32),
            pltpu.VMEM((2, span, ny), f32),
            pltpu.VMEM((2, tall, ny), f32),
            dma((5,)), dma((2, 5)), dma((2, 5)),
            dma((TOTAL,)), dma((TOTAL,)), dma((TOTAL,)), dma((TOTAL,)),
            dma, dma, dma, dma,
            dma((nx,)), dma((nx,)), dma((3, nx)),
        ],
        compiler_params=pltpu.CompilerParams(
            collective_id=collective, has_side_effects=True, vmem_limit_bytes=52 * 1024 * 1024),
    )(e_field, h_field, polar, polar_rate, material, shift_counts)


def local(e_field, h_field, polar, polar_rate, material, shift_counts):
    counts = list(range(SMAX + 8, CYCLES * SMAX + 1, 8))
    chosen = jnp.clip((shift_counts[0] + shift_counts[1] + 7) // 8 - counts[0] // 8, 0, len(counts) - 1)
    branches = [functools.partial(run, rows, k) for k, rows in enumerate(counts)]
    return tuple(lax.switch(chosen, branches, e_field, h_field, polar, polar_rate, material, shift_counts))


def solution(mesh):
    placed = (
        P(None, "ta", "gz", None),
        P(None, "ta", "gz", None),
        P(None, "ta", "gz", None),
        P(None, "ta", "gz", None),
        P("ta", "gz", None),
        P(),
    )
    return jax.shard_map(
        local,
        mesh=mesh,
        in_specs=placed,
        out_specs=(P(None, "ta", "gz", None), P(None, "ta", "gz", None), P(None, "ta", "gz", None)),
        check_vma=False,
    )
```
